32 devices in a mesh: grp: 2 (over y), row: 16 (over z, x, core), col: 1.
Axes of the slice: x: 2, y: 2, z: 4, core: 2. Of those that a mesh axis runs over, the one named last changes fastest.
Arguments:
- pair: bfloat16 [256, 128, 128], P(('grp', 'row'), 'col'), parts along dimension 0, may hold values from -6 to 6
- in_gain: float32 [2, 128], replicated, may hold values from 0.25 to 1.75
- in_shift: float32 [2, 128], replicated, may hold values from -3 to 3
- proj: bfloat16 [2, 128, 640], replicated, may hold values from -0.5 to 0.5
- out_gain: float32 [2, 128], replicated, may hold values from 0.25 to 1.75
- out_shift: float32 [2, 128], replicated, may hold values from -3 to 3
- out_weight: bfloat16 [2, 128, 128], replicated, may hold values from -0.5 to 0.5
Outputs:
- updated: bfloat16 [256, 128, 128], P(('grp', 'row'), 'col'), parts along dimension 0
The draws below stay inside these ranges and needn't reach their ends.
There are 2 independent parts, one for each index of `grp`. The reference program is written for one: setup_inputs(seed, part) draws one part's arguments, and reference() takes and returns one part's arrays. A program takes and returns all parts, laid end to end along the dimension named above; an argument that names none is the same for every part. Nothing has to cross between parts.
All inputs are finite; a program needn't handle non-finite values.
Results may differ from the reference program's by a relative error of at most 0.013.
Values may be sent and summed in bfloat16 or wider, within the bound.
A program may use at most 64 MiB of HBM per device.

```python
import jax
import jax.numpy as jnp
from jax import lax

C = 128
N = 128


def shard_levels(own_key, shape, shards, low, high):
    loudness, own = 1.0, jax.random.fold_in(own_key, 6)
    for axis_at, shards_of in shards:
        draws = jnp.exp(jax.random.uniform(jax.random.fold_in(own, axis_at), (shards_of,), jnp.float32, low / len(shards), high / len(shards)))
        loudness = loudness * jnp.repeat(draws, shape[axis_at] // shards_of).reshape([-1 if axis == axis_at else 1 for axis in range(len(shape))])
    return loudness


def normal_values(own_key, dims, deviation, reach, pieces=(), kind=jnp.bfloat16):
    entries = jax.random.normal(own_key, dims, jnp.float32) * deviation
    if len(pieces) > 0:
        entries = shard_levels(own_key, dims, pieces, -0.22, 0.18) * entries
    return jnp.clip(entries, min=-reach, max=reach).astype(kind)


def setup_inputs(seed: int = 0, part: int = 0) -> dict:
    streams_of = jax.random.split(jax.random.key(seed), 8)
    own_keys = jax.random.split(jax.random.fold_in(streams_of[7], part), 8)
    pair = normal_values(own_keys[0], (N, N, C), 1.0, 6.0, ((0, 16),))
    in_gain = jnp.clip(1.0 + 0.15 * jax.random.normal(streams_of[1], (2, C), jnp.float32), 0.25, 1.75)
    in_shift = normal_values(streams_of[2], (2, C), 0.5, 3.0, (), jnp.float32)
    proj = normal_values(streams_of[3], (2, C, 5 * C), C ** -0.5, 0.5)
    out_gain = jnp.clip(1.0 + 0.15 * jax.random.normal(streams_of[4], (2, C), jnp.float32), 0.25, 1.75)
    out_shift = normal_values(streams_of[5], (2, C), 0.5, 3.0, (), jnp.float32)
    out_weight = normal_values(streams_of[6], (2, C, C), C ** -0.5, 0.5)
    return {"pair": pair, "in_gain": in_gain, "in_shift": in_shift, "proj": proj, "out_gain": out_gain, "out_shift": out_shift, "out_weight": out_weight}


def layer_norm(values, scale_vec, offset):
    average = lax.optimization_barrier(jnp.mean(values, axis=-1, keepdims=True))
    centred = values - average
    variance = lax.optimization_barrier(jnp.mean(centred * centred, axis=-1, keepdims=True))
    return centred * lax.rsqrt(variance + 1e-05) * scale_vec + offset

def reference(pair, in_gain, in_shift, proj, out_gain, out_shift, out_weight):
    block_rows = 8
    count_blocks = N // block_rows
    current = pair
    for layer_index in range(2):
        weights = proj[layer_index].astype(jnp.float32)

        def project_rows(rows):
            normed = layer_norm(rows.astype(jnp.float32), in_gain[layer_index], in_shift[layer_index]).astype(jnp.bfloat16)
            projected = jnp.einsum('ijc,cd->ijd', normed.astype(jnp.float32), weights)
            left_edge = (jax.nn.sigmoid(projected[..., C:2 * C]) * projected[..., :C]).astype(jnp.bfloat16)
            right_edge = (jax.nn.sigmoid(projected[..., 3 * C:4 * C]) * projected[..., 2 * C:3 * C]).astype(jnp.bfloat16)
            out_gate = jax.nn.sigmoid(projected[..., 4 * C:])
            return (left_edge, right_edge, out_gate)
        left_edge, right_edge, out_gate = lax.map(project_rows, current.reshape(count_blocks, block_rows, N, C))
        left_edge = left_edge.reshape(N, N, C).transpose(2, 0, 1)
        right_edge = right_edge.reshape(N, N, C).transpose(2, 0, 1)
        out_gate = out_gate.reshape(N, N, C)

        def contract(operands):
            first_edge = operands[0].astype(jnp.float32)
            second_edge = operands[1].astype(jnp.float32)
            if layer_index == 0:
                result = jnp.einsum('cik,cjk->cij', first_edge, second_edge)
            else:
                result = jnp.einsum('cki,ckj->cij', first_edge, second_edge)
            return result.astype(jnp.bfloat16)
        group = 8
        product = lax.map(contract, (left_edge.reshape(C // group, group, N, N), right_edge.reshape(C // group, group, N, N)))
        product = product.reshape(C, N, N).transpose(1, 2, 0)
        out_mat = out_weight[layer_index].astype(jnp.float32)

        def finish_rows(operands):
            rows, prod_rows, gate_rows = operands
            product_norm = layer_norm(prod_rows.astype(jnp.float32), out_gain[layer_index], out_shift[layer_index]).astype(jnp.bfloat16)
            update = jnp.einsum('ijc,cd->ijd', product_norm.astype(jnp.float32), out_mat) * gate_rows
            return (rows.astype(jnp.float32) + update).astype(jnp.bfloat16)
        current = lax.map(finish_rows, (current.reshape(count_blocks, block_rows, N, C), product.reshape(count_blocks, block_rows, N, C), out_gate.reshape(count_blocks, block_rows, N, C))).reshape(N, N, C)
    return current
```

```python
import functools

import jax
import jax.numpy as jnp
from jax import lax
from jax.experimental import pallas as pl
from jax.experimental.pallas import tpu as pltpu
from jax.sharding import PartitionSpec as P


def layer_norm(values, scale_vec, offset, axis_pos):
    average = jnp.mean(values, axis=axis_pos, keepdims=True)
    centred = values - average
    variance = jnp.mean(centred * centred, axis=axis_pos, keepdims=True)
    return centred * lax.rsqrt(variance + 1e-05) * scale_vec + offset


def arrange_blocks(arrived, row_count, col_count):
    sources, local_chan, rows_here, cols_here = arrived.shape
    shaped = arrived.reshape(row_count, col_count, local_chan, rows_here, cols_here)
    shaped = shaped.transpose(2, 0, 3, 1, 4)
    return shaped.reshape(local_chan, row_count * rows_here, col_count * cols_here)


def plain_body(pair, in_gain, in_shift, proj, out_gain, out_shift, out_weight):
    rows_here, cols_here, channels = pair.shape
    row_count = lax.axis_size("row")
    col_count = lax.axis_size("col")
    local_chan = channels // (row_count * col_count)
    current = pair
    for layer_index in range(2):
        normed = layer_norm(
            current.astype(jnp.float32), in_gain[layer_index], in_shift[layer_index], 2
        ).astype(jnp.bfloat16)
        weights = proj[layer_index]
        projected = jnp.einsum(
            "ijc,cd->dij", normed, weights[:, : 4 * channels], preferred_element_type=jnp.float32
        )
        left_edge = (
            jax.nn.sigmoid(projected[channels : 2 * channels]) * projected[:channels]
        ).astype(jnp.bfloat16)
        right_edge = (
            jax.nn.sigmoid(projected[3 * channels :]) * projected[2 * channels : 3 * channels]
        ).astype(jnp.bfloat16)
        out_gate = jax.nn.sigmoid(
            jnp.einsum(
                "ijc,cd->ijd",
                normed,
                weights[:, 4 * channels :],
                preferred_element_type=jnp.float32,
            )
        )
        left_arrived, right_arrived = (
            lax.all_to_all(
                left_edge[None], ("row", "col"), split_axis=1, concat_axis=0, tiled=True
            ),
            lax.all_to_all(
                right_edge[None], ("row", "col"), split_axis=1, concat_axis=0, tiled=True
            ),
        )
        left_full = arrange_blocks(left_arrived, row_count, col_count)
        right_full = arrange_blocks(right_arrived, row_count, col_count)
        if layer_index == 0:
            product = jnp.einsum(
                "cik,cjk->cij", left_full, right_full, preferred_element_type=jnp.float32
            )
        else:
            product = jnp.einsum(
                "cki,ckj->cij", left_full, right_full, preferred_element_type=jnp.float32
            )
        product = product.astype(jnp.bfloat16)
        outgoing = product.reshape(local_chan, row_count, rows_here, col_count, cols_here)
        outgoing = outgoing.transpose(1, 3, 0, 2, 4).reshape(
            row_count * col_count, local_chan, rows_here, cols_here
        )
        returned = lax.all_to_all(outgoing, ("row", "col"), split_axis=0, concat_axis=1, tiled=True)
        returned = returned.reshape(channels, rows_here, cols_here)
        product_norm = layer_norm(
            returned.astype(jnp.float32),
            out_gain[layer_index][:, None, None],
            out_shift[layer_index][:, None, None],
            0,
        ).astype(jnp.bfloat16)
        update = (
            jnp.einsum(
                "cij,cd->ijd",
                product_norm,
                out_weight[layer_index],
                preferred_element_type=jnp.float32,
            )
            * out_gate
        )
        current = (current.astype(jnp.float32) + update).astype(jnp.bfloat16)
    return current


PARTS = 2
TOKENS = 128
CHANNELS = 128
ROWS = 8


def sigmoid(values):
    return 0.5 * jnp.tanh(0.5 * values) + 0.5


def kernel(
    n, pair_ref, in_gain, in_shift, proj, out_gain, out_shift, out_weight, out_ref,
    weights_t, normed, gate, current, edges, centred, send, recv, ret, got, send_sem, recv_sem,
):
    me = lax.axis_index("row")
    part_chan = CHANNELS // PARTS
    local = part_chan // n
    cells = ROWS * TOKENS

    def copy(layer, phase, part, source, target, offset):
        dst = lax.rem(me + offset, n)
        return pltpu.make_async_remote_copy(
            src_ref=source.at[layer, part, dst],
            dst_ref=target.at[layer, part, me],
            send_sem=send_sem.at[layer, phase, part],
            recv_sem=recv_sem.at[layer, phase, part],
            device_id={"row": dst},
            device_id_type=pl.DeviceIdType.MESH,
        )

    def start_all(layer, phase, part, source, target):
        def step(offset, carry):
            copy(layer, phase, part, source, target, offset).start()
            return carry

        lax.fori_loop(1, n, step, 0, unroll=True)
        target[layer, part, me] = source[layer, part, me]

    def wait_all(sems, layer, phase, part, buffer):
        blocks = buffer.at[layer, part, pl.ds(0, n - 1)]
        pltpu.make_async_copy(blocks, blocks, sems.at[layer, phase, part]).wait()

    barrier = pltpu.get_barrier_semaphore()

    def greet(offset, carry):
        pl.semaphore_signal(
            barrier, inc=1, device_id={"row": lax.rem(me + offset, n)},
            device_id_type=pl.DeviceIdType.MESH,
        )
        return carry

    lax.fori_loop(1, n, greet, 0)

    for layer in range(2):
        for block in range(4):
            columns = proj[layer, :, block * CHANNELS : (block + 1) * CHANNELS]
            turned = columns.astype(jnp.float32).T.astype(jnp.bfloat16)
            for part in range(PARTS):
                weights_t[layer, part, block * part_chan : (block + 1) * part_chan, :] = turned[
                    part * part_chan : (part + 1) * part_chan
                ]

    for layer in range(2):
        source = pair_ref if layer == 0 else current
        for i in range(ROWS):
            rows = source[i].astype(jnp.float32)
            average = jnp.mean(rows, axis=-1, keepdims=True)
            shifted = rows - average
            variance = jnp.mean(shifted * shifted, axis=-1, keepdims=True)
            normed[i] = (
                shifted * lax.rsqrt(variance + 1e-05) * in_gain[layer][None] + in_shift[layer][None]
            ).astype(jnp.bfloat16)
        for part in range(PARTS):
            for i in range(ROWS):
                projected = lax.dot_general(
                    weights_t[layer, part], normed[i], (((1,), (1,)), ((), ())),
                    preferred_element_type=jnp.float32,
                )
                p1, p2, p3, p4 = (
                    projected[b * part_chan : (b + 1) * part_chan] for b in range(4)
                )
                edges[part, pl.ds(i, part_chan, stride=2 * ROWS), :] = sigmoid(p2) * p1
                edges[part, pl.ds(ROWS + i, part_chan, stride=2 * ROWS), :] = sigmoid(p4) * p3
            send[layer, part] = (
                edges[part].astype(jnp.bfloat16).reshape(n, local, 2 * ROWS, TOKENS)
            )
            if layer == 0 and part == 0:
                pl.semaphore_wait(barrier, n - 1)
            start_all(layer, 0, part, send, recv)
        for i in range(ROWS):
            gate[i] = sigmoid(
                jnp.dot(
                    normed[i], proj[layer, :, 4 * CHANNELS :], preferred_element_type=jnp.float32
                )
            )
        for part in range(PARTS):
            wait_all(recv_sem, layer, 0, part, recv)
            for pair_at in range(local // 2):
                products = []
                for channel in (2 * pair_at, 2 * pair_at + 1):
                    both = recv[layer, part, :, channel].astype(jnp.float32)
                    left = both[:, :ROWS].reshape(TOKENS, TOKENS).astype(jnp.bfloat16)
                    right = both[:, ROWS:].reshape(TOKENS, TOKENS).astype(jnp.bfloat16)
                    dims = ((1,), (1,)) if layer == 0 else ((0,), (0,))
                    product = lax.dot_general(
                        left, right, (dims, ((), ())), preferred_element_type=jnp.float32
                    )
                    products.append(product.reshape(n, ROWS, TOKENS))
                ret[layer, part, :, pair_at] = jnp.concatenate(products, axis=1).astype(
                    jnp.bfloat16
                )
            start_all(layer, 1, part, ret, got)
        total = jnp.zeros((ROWS, TOKENS), jnp.float32)
        for part in range(PARTS):
            wait_all(recv_sem, layer, 1, part, got)
            values = got[layer, part].astype(jnp.float32).reshape(part_chan, ROWS, TOKENS)
            first = part * part_chan * ROWS
            centred[first : first + part_chan * ROWS] = values.reshape(part_chan * ROWS, TOKENS)
            total += jnp.sum(values, axis=0)
        average = total / CHANNELS
        shifted = centred[...].reshape(CHANNELS, ROWS, TOKENS) - average[None]
        variance = jnp.mean(shifted * shifted, axis=0)
        scaled = shifted * lax.rsqrt(variance + 1e-05)[None]
        centred[...] = scaled.reshape(CHANNELS * ROWS, TOKENS)
        for i in range(ROWS):
            turned = centred[pl.ds(i, CHANNELS, stride=ROWS), :].T
            product_norm = (turned * out_gain[layer][None] + out_shift[layer][None]).astype(
                jnp.bfloat16
            )
            update = (
                jnp.dot(product_norm, out_weight[layer], preferred_element_type=jnp.float32)
                * gate[i]
            )
            target = current if layer == 0 else out_ref
            target[i] = (source[i].astype(jnp.float32) + update).astype(jnp.bfloat16)
    for layer in range(2):
        for part in range(PARTS):
            wait_all(send_sem, layer, 0, part, send)
            wait_all(send_sem, layer, 1, part, ret)


def kernel_body(n, *arrays):
    part_chan = CHANNELS // PARTS
    local = part_chan // n
    edge_blocks = (2, PARTS, n, local, 2 * ROWS, TOKENS)
    product_blocks = (2, PARTS, n, local // 2, 2 * ROWS, TOKENS)
    vmem = pl.BlockSpec(memory_space=pltpu.VMEM)
    return pl.pallas_call(
        functools.partial(kernel, n),
        out_shape=jax.ShapeDtypeStruct((ROWS, TOKENS, CHANNELS), jnp.bfloat16),
        in_specs=[vmem] * 7,
        out_specs=vmem,
        scratch_shapes=[
            pltpu.VMEM((2, PARTS, 4 * part_chan, CHANNELS), jnp.bfloat16),
            pltpu.VMEM((ROWS, TOKENS, CHANNELS), jnp.bfloat16),
            pltpu.VMEM((ROWS, TOKENS, CHANNELS), jnp.float32),
            pltpu.VMEM((ROWS, TOKENS, CHANNELS), jnp.bfloat16),
            pltpu.VMEM((PARTS, part_chan * 2 * ROWS, TOKENS), jnp.float32),
            pltpu.VMEM((CHANNELS * ROWS, TOKENS), jnp.float32),
            pltpu.VMEM(edge_blocks, jnp.bfloat16),
            pltpu.VMEM(edge_blocks, jnp.bfloat16),
            pltpu.VMEM(product_blocks, jnp.bfloat16),
            pltpu.VMEM(product_blocks, jnp.bfloat16),
            pltpu.SemaphoreType.DMA((2, 2, PARTS)),
            pltpu.SemaphoreType.DMA((2, 2, PARTS)),
        ],
        compiler_params=pltpu.CompilerParams(
            collective_id=0, has_side_effects=True, vmem_limit_bytes=48 * 1024 * 1024
        ),
    )(*arrays)


def body(pair, *params):
    n = lax.axis_size("row")
    fits = (
        lax.axis_size("col") == 1
        and pair.shape == (ROWS, TOKENS, CHANNELS)
        and n * ROWS == TOKENS
        and CHANNELS % (2 * n * PARTS) == 0
    )
    if fits:
        return kernel_body(n, pair, *params)
    return plain_body(pair, *params)


def solution(mesh):
    placed = (P(("grp", "row"), "col", None), P(), P(), P(), P(), P(), P())
    return jax.shard_map(
        body, mesh=mesh, in_specs=placed, out_specs=P(("grp", "row"), "col", None), check_vma=False
    )
```

```python
import functools

import jax
import jax.numpy as jnp
from jax import lax
from jax.experimental import pallas as pl
from jax.experimental.pallas import tpu as pltpu
from jax.sharding import PartitionSpec as P


def layer_norm(values, scale_vec, offset, axis_pos):
    average = jnp.mean(values, axis=axis_pos, keepdims=True)
    centred = values - average
    variance = jnp.mean(centred * centred, axis=axis_pos, keepdims=True)
    return centred * lax.rsqrt(variance + 1e-05) * scale_vec + offset


def arrange_blocks(arrived, row_count, col_count):
    sources, local_chan, rows_here, cols_here = arrived.shape
    shaped = arrived.reshape(row_count, col_count, local_chan, rows_here, cols_here)
    shaped = shaped.transpose(2, 0, 3, 1, 4)
    return shaped.reshape(local_chan, row_count * rows_here, col_count * cols_here)


def plain_body(pair, in_gain, in_shift, proj, out_gain, out_shift, out_weight):
    rows_here, cols_here, channels = pair.shape
    row_count = lax.axis_size("row")
    col_count = lax.axis_size("col")
    local_chan = channels // (row_count * col_count)
    current = pair
    for layer_index in range(2):
        normed = layer_norm(
            current.astype(jnp.float32), in_gain[layer_index], in_shift[layer_index], 2
        ).astype(jnp.bfloat16)
        weights = proj[layer_index]
        projected = jnp.einsum(
            "ijc,cd->dij", normed, weights[:, : 4 * channels], preferred_element_type=jnp.float32
        )
        left_edge = (
            jax.nn.sigmoid(projected[channels : 2 * channels]) * projected[:channels]
        ).astype(jnp.bfloat16)
        right_edge = (
            jax.nn.sigmoid(projected[3 * channels :]) * projected[2 * channels : 3 * channels]
        ).astype(jnp.bfloat16)
        out_gate = jax.nn.sigmoid(
            jnp.einsum(
                "ijc,cd->ijd",
                normed,
                weights[:, 4 * channels :],
                preferred_element_type=jnp.float32,
            )
        )
        left_arrived, right_arrived = (
            lax.all_to_all(
                left_edge[None], ("row", "col"), split_axis=1, concat_axis=0, tiled=True
            ),
            lax.all_to_all(
                right_edge[None], ("row", "col"), split_axis=1, concat_axis=0, tiled=True
            ),
        )
        left_full = arrange_blocks(left_arrived, row_count, col_count)
        right_full = arrange_blocks(right_arrived, row_count, col_count)
        if layer_index == 0:
            product = jnp.einsum(
                "cik,cjk->cij", left_full, right_full, preferred_element_type=jnp.float32
            )
        else:
            product = jnp.einsum(
                "cki,ckj->cij", left_full, right_full, preferred_element_type=jnp.float32
            )
        product = product.astype(jnp.bfloat16)
        outgoing = product.reshape(local_chan, row_count, rows_here, col_count, cols_here)
        outgoing = outgoing.transpose(1, 3, 0, 2, 4).reshape(
            row_count * col_count, local_chan, rows_here, cols_here
        )
        returned = lax.all_to_all(outgoing, ("row", "col"), split_axis=0, concat_axis=1, tiled=True)
        returned = returned.reshape(channels, rows_here, cols_here)
        product_norm = layer_norm(
            returned.astype(jnp.float32),
            out_gain[layer_index][:, None, None],
            out_shift[layer_index][:, None, None],
            0,
        ).astype(jnp.bfloat16)
        update = (
            jnp.einsum(
                "cij,cd->ijd",
                product_norm,
                out_weight[layer_index],
                preferred_element_type=jnp.float32,
            )
            * out_gate
        )
        current = (current.astype(jnp.float32) + update).astype(jnp.bfloat16)
    return current


PARTS = (1, 2)
TOKENS = 128
CHANNELS = 128
ROWS = 8


def sigmoid(values):
    return 0.5 * jnp.tanh(0.5 * values) + 0.5


def kernel(n, *refs):
    hbm, out_ref, vmem, rest = refs[:7], refs[7], refs[8:15], refs[15:]
    pair_ref, in_gain, in_shift, proj, out_gain, out_shift, out_weight = vmem
    load_sem, weights_t, normed, gate, current, edges, centred, send_sem, recv_sem = rest[:9]
    buffers = rest[9:]
    loads = [
        pltpu.make_async_copy(hbm[at], vmem[at], load_sem.at[at]) for at in (0, 3, 1, 2, 4, 5, 6)
    ]
    for load in loads:
        load.start()
    me = lax.axis_index("row")
    half = n // 2
    side, place = me // half, lax.rem(me, half)

    def start(source, target, sems, device):
        pltpu.make_async_remote_copy(
            src_ref=source,
            dst_ref=target,
            send_sem=send_sem.at[sems],
            recv_sem=recv_sem.at[sems],
            device_id={"row": device},
            device_id_type=pl.DeviceIdType.MESH,
        ).start()

    def start_half(source, target, sems, slot):
        for offset in range(1, half):
            other = lax.rem(place + offset, half)
            start(source.at[other], target.at[slot], sems, side * half + other)
        target[slot] = source[place]

    def wait_all(sem, buffer, count):
        blocks = buffer.at[pl.ds(0, count)]
        pltpu.make_async_copy(blocks, blocks, sem).wait()

    barrier = pltpu.get_barrier_semaphore()

    def greet(offset, carry):
        pl.semaphore_signal(
            barrier, inc=1, device_id={"row": lax.rem(me + offset, n)},
            device_id_type=pl.DeviceIdType.MESH,
        )
        return carry

    lax.fori_loop(1, n, greet, 0)

    loads[1].wait()
    for layer in range(2):
        part_chan = CHANNELS // PARTS[layer]
        for block in range(4):
            columns = proj[layer, :, block * CHANNELS : (block + 1) * CHANNELS]
            turned = columns.astype(jnp.float32).T.astype(jnp.bfloat16)
            for part in range(PARTS[layer]):
                weights_t[
                    layer, pl.ds((4 * part + block) * part_chan, part_chan), :
                ] = turned[part * part_chan : (part + 1) * part_chan]
    for load in (loads[0], loads[2], loads[3]):
        load.wait()
    for layer in range(2):
        parts = PARTS[layer]
        part_chan = CHANNELS // parts
        pairs = part_chan // half // 2
        send, recv, ret, got = buffers[4 * layer : 4 * layer + 4]
        source = pair_ref if layer == 0 else current
        for i in range(ROWS):
            rows = source[i].astype(jnp.float32)
            average = jnp.mean(rows, axis=-1, keepdims=True)
            shifted = rows - average
            variance = jnp.mean(shifted * shifted, axis=-1, keepdims=True)
            normed[i] = (
                shifted * lax.rsqrt(variance + 1e-05) * in_gain[layer][None] + in_shift[layer][None]
            ).astype(jnp.bfloat16)
        for part in range(parts):
            for i in range(ROWS):
                projected = lax.dot_general(
                    weights_t[layer, pl.ds(4 * part * part_chan, 4 * part_chan), :],
                    normed[i], (((1,), (1,)), ((), ())),
                    preferred_element_type=jnp.float32,
                )
                p1, p2, p3, p4 = (
                    projected[b * part_chan : (b + 1) * part_chan] for b in range(4)
                )
                edges[0, pl.ds(i, part_chan, stride=ROWS), :] = sigmoid(p2) * p1
                edges[1, pl.ds(i, part_chan, stride=ROWS), :] = sigmoid(p4) * p3
            for edge in range(2):
                send[part, :, edge] = (
                    edges[edge, : part_chan * ROWS]
                    .astype(jnp.bfloat16)
                    .reshape(half, pairs, 2 * ROWS, TOKENS)
                )
            sems = (layer, 0, part)
            if layer == 0 and part == 0:
                pl.semaphore_wait(barrier, n - 1)
            if layer == 0:
                for offset in range(half):
                    other = lax.rem(place + offset, half)
                    start(
                        send.at[part, other, 1], recv.at[part, me, 1], sems,
                        (1 - side) * half + other,
                    )
                start_half(send.at[part], recv.at[part], sems, me)
            else:
                start_half(send.at[part], recv.at[part], sems, place)
        for i in range(ROWS):
            gate[i] = sigmoid(
                jnp.dot(
                    normed[i], proj[layer, :, 4 * CHANNELS :], preferred_element_type=jnp.float32
                )
            )
        for part in range(parts):
            count = half // 2 + half - 1 if layer == 0 else half - 1
            wait_all(recv_sem.at[layer, 0, part], recv.at[part], count)
            own = pl.ds(side * half, half) if layer == 0 else slice(None)
            for pair_at in range(pairs):
                left = recv[part, own, 0, pair_at].astype(jnp.float32)
                right = recv[part, :, 1, pair_at].astype(jnp.float32)
                products = []
                for rows in (slice(0, ROWS), slice(ROWS, 2 * ROWS)):
                    product = lax.dot_general(
                        left[:, rows].reshape(-1, TOKENS).astype(jnp.bfloat16),
                        right[:, rows].reshape(-1, TOKENS).astype(jnp.bfloat16),
                        (((1,), (1,)) if layer == 0 else ((0,), (0,)), ((), ())),
                        preferred_element_type=jnp.float32,
                    )
                    products.append(product.reshape(-1, ROWS, TOKENS))
                ret[part, :, pair_at] = jnp.concatenate(products, axis=1).astype(jnp.bfloat16)
            sems = (layer, 1, part)
            if layer == 0:
                start_half(ret.at[part], got.at[part], sems, place)
            else:
                for offset in range(1, n):
                    other = lax.rem(me + offset, n)
                    start(ret.at[part, other], got.at[part, me], sems, other)
                got[part, me] = ret[part, me]
        if layer == 0:
            for load in loads[4:]:
                load.wait()
        total = jnp.zeros((ROWS, TOKENS), jnp.float32)
        for part in range(parts):
            wait_all(recv_sem.at[layer, 1, part], got.at[part], (half if layer == 0 else n) - 1)
            values = got[part].astype(jnp.float32)
            if layer == 1:
                values = values[:half] + values[half:]
            values = values.reshape(part_chan, ROWS, TOKENS)
            first = part * part_chan * ROWS
            centred[first : first + part_chan * ROWS] = values.reshape(part_chan * ROWS, TOKENS)
            total += jnp.sum(values, axis=0)
        average = total / CHANNELS
        shifted = centred[...].reshape(CHANNELS, ROWS, TOKENS) - average[None]
        variance = jnp.mean(shifted * shifted, axis=0)
        scaled = shifted * lax.rsqrt(variance + 1e-05)[None]
        centred[...] = scaled.reshape(CHANNELS * ROWS, TOKENS)
        for i in range(ROWS):
            turned = centred[pl.ds(i, CHANNELS, stride=ROWS), :].T
            product_norm = (turned * out_gain[layer][None] + out_shift[layer][None]).astype(
                jnp.bfloat16
            )
            update = (
                jnp.dot(product_norm, out_weight[layer], preferred_element_type=jnp.float32)
                * gate[i]
            )
            target = current if layer == 0 else out_ref
            target[i] = (source[i].astype(jnp.float32) + update).astype(jnp.bfloat16)
    for layer in range(2):
        send, recv, ret, got = buffers[4 * layer : 4 * layer + 4]
        for part in range(PARTS[layer]):
            count = half // 2 + half - 1 if layer == 0 else half - 1
            wait_all(send_sem.at[layer, 0, part], recv.at[part], count)
            wait_all(send_sem.at[layer, 1, part], got.at[part], (half if layer == 0 else n) - 1)


def kernel_body(n, *arrays):
    half = n // 2
    blocks = []
    for layer in range(2):
        parts = PARTS[layer]
        tiles = (CHANNELS // parts // half // 2, 2 * ROWS, TOKENS)
        blocks += [
            (parts, half, 2) + tiles,
            (parts, n if layer == 0 else half, 2) + tiles,
            (parts, half if layer == 0 else n) + tiles,
            (parts, half if layer == 0 else n) + tiles,
        ]
    return pl.pallas_call(
        functools.partial(kernel, n),
        out_shape=jax.ShapeDtypeStruct((ROWS, TOKENS, CHANNELS), jnp.bfloat16),
        in_specs=[pl.BlockSpec(memory_space=pltpu.HBM)] * 7,
        out_specs=pl.BlockSpec(memory_space=pltpu.VMEM),
        scratch_shapes=[pltpu.VMEM(array.shape, array.dtype) for array in arrays]
        + [
            pltpu.SemaphoreType.DMA((7,)),
            pltpu.VMEM((2, 4 * CHANNELS, CHANNELS), jnp.bfloat16),
            pltpu.VMEM((ROWS, TOKENS, CHANNELS), jnp.bfloat16),
            pltpu.VMEM((ROWS, TOKENS, CHANNELS), jnp.float32),
            pltpu.VMEM((ROWS, TOKENS, CHANNELS), jnp.bfloat16),
            pltpu.VMEM((2, CHANNELS * ROWS, TOKENS), jnp.float32),
            pltpu.VMEM((CHANNELS * ROWS, TOKENS), jnp.float32),
            pltpu.SemaphoreType.DMA((2, 2, max(PARTS))),
            pltpu.SemaphoreType.DMA((2, 2, max(PARTS))),
        ]
        + [pltpu.VMEM(block, jnp.bfloat16) for block in blocks],
        compiler_params=pltpu.CompilerParams(collective_id=0, has_side_effects=True),
    )(*arrays)


def body(pair, *params):
    n = lax.axis_size("row")
    fits = (
        lax.axis_size("col") == 1
        and pair.shape == (ROWS, TOKENS, CHANNELS)
        and n * ROWS == TOKENS
        and n % 4 == 0
        and all(CHANNELS % (n * parts) == 0 for parts in PARTS)
    )
    if fits:
        return kernel_body(n, pair, *params)
    return plain_body(pair, *params)


def solution(mesh):
    placed = (P(("grp", "row"), "col", None), P(), P(), P(), P(), P(), P())
    return jax.shard_map(
        body, mesh=mesh, in_specs=placed, out_specs=P(("grp", "row"), "col", None), check_vma=False
    )
```

```python
import functools

import jax
import jax.numpy as jnp
from jax import lax
from jax.experimental import pallas as pl
from jax.experimental.pallas import tpu as pltpu
from jax.sharding import PartitionSpec as P


def layer_norm(values, scale_vec, offset, axis_pos):
    average = jnp.mean(values, axis=axis_pos, keepdims=True)
    centred = values - average
    variance = jnp.mean(centred * centred, axis=axis_pos, keepdims=True)
    return centred * lax.rsqrt(variance + 1e-05) * scale_vec + offset


def arrange_blocks(arrived, row_count, col_count):
    sources, local_chan, rows_here, cols_here = arrived.shape
    shaped = arrived.reshape(row_count, col_count, local_chan, rows_here, cols_here)
    shaped = shaped.transpose(2, 0, 3, 1, 4)
    return shaped.reshape(local_chan, row_count * rows_here, col_count * cols_here)


def plain_body(pair, in_gain, in_shift, proj, out_gain, out_shift, out_weight):
    rows_here, cols_here, channels = pair.shape
    row_count = lax.axis_size("row")
    col_count = lax.axis_size("col")
    local_chan = channels // (row_count * col_count)
    current = pair
    for layer_index in range(2):
        normed = layer_norm(
            current.astype(jnp.float32), in_gain[layer_index], in_shift[layer_index], 2
        ).astype(jnp.bfloat16)
        weights = proj[layer_index]
        projected = jnp.einsum(
            "ijc,cd->dij", normed, weights[:, : 4 * channels], preferred_element_type=jnp.float32
        )
        left_edge = (
            jax.nn.sigmoid(projected[channels : 2 * channels]) * projected[:channels]
        ).astype(jnp.bfloat16)
        right_edge = (
            jax.nn.sigmoid(projected[3 * channels :]) * projected[2 * channels : 3 * channels]
        ).astype(jnp.bfloat16)
        out_gate = jax.nn.sigmoid(
            jnp.einsum(
                "ijc,cd->ijd",
                normed,
                weights[:, 4 * channels :],
                preferred_element_type=jnp.float32,
            )
        )
        left_arrived, right_arrived = (
            lax.all_to_all(
                left_edge[None], ("row", "col"), split_axis=1, concat_axis=0, tiled=True
            ),
            lax.all_to_all(
                right_edge[None], ("row", "col"), split_axis=1, concat_axis=0, tiled=True
            ),
        )
        left_full = arrange_blocks(left_arrived, row_count, col_count)
        right_full = arrange_blocks(right_arrived, row_count, col_count)
        if layer_index == 0:
            product = jnp.einsum(
                "cik,cjk->cij", left_full, right_full, preferred_element_type=jnp.float32
            )
        else:
            product = jnp.einsum(
                "cki,ckj->cij", left_full, right_full, preferred_element_type=jnp.float32
            )
        product = product.astype(jnp.bfloat16)
        outgoing = product.reshape(local_chan, row_count, rows_here, col_count, cols_here)
        outgoing = outgoing.transpose(1, 3, 0, 2, 4).reshape(
            row_count * col_count, local_chan, rows_here, cols_here
        )
        returned = lax.all_to_all(outgoing, ("row", "col"), split_axis=0, concat_axis=1, tiled=True)
        returned = returned.reshape(channels, rows_here, cols_here)
        product_norm = layer_norm(
            returned.astype(jnp.float32),
            out_gain[layer_index][:, None, None],
            out_shift[layer_index][:, None, None],
            0,
        ).astype(jnp.bfloat16)
        update = (
            jnp.einsum(
                "cij,cd->ijd",
                product_norm,
                out_weight[layer_index],
                preferred_element_type=jnp.float32,
            )
            * out_gate
        )
        current = (current.astype(jnp.float32) + update).astype(jnp.bfloat16)
    return current


PARTS = ((("half", 96), ("half", 32)), (("half", 64), ("all", 64)))
TOKENS = 128
CHANNELS = 128
ROWS = 8


def sigmoid(values):
    return 0.5 * jnp.tanh(0.5 * values) + 0.5


def kernel(n, *refs):
    hbm, out_ref, vmem, rest = refs[:7], refs[7], refs[8:15], refs[15:]
    pair_ref, in_gain, in_shift, proj, out_gain, out_shift, out_weight = vmem
    load_sem, weights_t, normed, gate, current, edges, centred, send_sem, recv_sem = rest[:9]
    buffers, at = [], 9
    for layer in range(2):
        buffers.append([rest[at + 4 * part : at + 4 * part + 4] for part in range(len(PARTS[layer]))])
        at += 4 * len(PARTS[layer])
    me = lax.axis_index("row")
    half = n // 2
    side, place = me // half, lax.rem(me, half)

    def start(source, target, sems, device):
        pltpu.make_async_remote_copy(
            src_ref=source,
            dst_ref=target,
            send_sem=send_sem.at[sems],
            recv_sem=recv_sem.at[sems],
            device_id={"row": device},
            device_id_type=pl.DeviceIdType.MESH,
        ).start()

    def start_group(source, target, sems):
        for offset in range(1, n):
            other = lax.rem(me + offset, n)
            start(source.at[other], target.at[me], sems, other)
        target[me] = source[me]

    def start_half(source, target, sems, slot):
        for offset in range(1, half):
            other = lax.rem(place + offset, half)
            start(source.at[other], target.at[slot], sems, side * half + other)
        target[slot] = source[place]

    def wait_all(sem, buffer, count):
        blocks = buffer.at[pl.ds(0, count)]
        pltpu.make_async_copy(blocks, blocks, sem).wait()

    def arriving(layer, kind):
        if kind == "all":
            return n - 1, n - 1
        return (half // 2 + half - 1, half - 1) if layer == 0 else (half - 1, n - 1)

    def start_edges(layer, part):
        send, recv, _, _ = buffers[layer][part]
        sems = (layer, 0, part)
        if PARTS[layer][part][0] == "all":
            start_group(send, recv, sems)
        elif layer == 0:
            for offset in range(half):
                other = lax.rem(place + offset, half)
                start(send.at[other, 1], recv.at[me, 1], sems, (1 - side) * half + other)
            start_half(send, recv, sems, me)
        else:
            start_half(send, recv, sems, place)

    barrier = pltpu.get_barrier_semaphore()

    def greet(offset, carry):
        pl.semaphore_signal(
            barrier, inc=1, device_id={"row": lax.rem(me + offset, n)},
            device_id_type=pl.DeviceIdType.MESH,
        )
        return carry

    lax.fori_loop(1, n, greet, 0)
    loads = [
        pltpu.make_async_copy(hbm[at], vmem[at], load_sem.at[at]) for at in (0, 3, 1, 2, 4, 5, 6)
    ]
    for load in loads:
        load.start()

    loads[1].wait()
    for layer in range(2):
        for block in range(4):
            columns = proj[layer, :, block * CHANNELS : (block + 1) * CHANNELS]
            turned = columns.astype(jnp.float32).T.astype(jnp.bfloat16)
            first = 0
            for _, count in PARTS[layer]:
                weights_t[layer, pl.ds(4 * first + block * count, count), :] = turned[
                    first : first + count
                ]
                first += count
    for load in (loads[0], loads[2], loads[3]):
        load.wait()
    for layer in range(2):
        parts = PARTS[layer]
        source = pair_ref if layer == 0 else current
        for i in range(ROWS):
            rows = source[i].astype(jnp.float32)
            average = jnp.mean(rows, axis=-1, keepdims=True)
            shifted = rows - average
            variance = jnp.mean(shifted * shifted, axis=-1, keepdims=True)
            normed[i] = (
                shifted * lax.rsqrt(variance + 1e-05) * in_gain[layer][None] + in_shift[layer][None]
            ).astype(jnp.bfloat16)
        first = 0
        for part, (kind, count) in enumerate(parts):
            send, recv, ret, got = buffers[layer][part]
            for i in range(ROWS):
                projected = lax.dot_general(
                    weights_t[layer, pl.ds(4 * first, 4 * count), :],
                    normed[i], (((1,), (1,)), ((), ())),
                    preferred_element_type=jnp.float32,
                )
                p1, p2, p3, p4 = (projected[b * count : (b + 1) * count] for b in range(4))
                edges[0, pl.ds(i, count, stride=ROWS), :] = sigmoid(p2) * p1
                edges[1, pl.ds(i, count, stride=ROWS), :] = sigmoid(p4) * p3
            for edge in range(2):
                send[:, edge] = (
                    edges[edge, : count * ROWS]
                    .astype(jnp.bfloat16)
                    .reshape(send.shape[0], send.shape[2], 2 * ROWS, TOKENS)
                )
            if layer == 1:
                start_edges(layer, part)
            first += count
        for i in range(ROWS):
            gate[i] = sigmoid(
                jnp.dot(
                    normed[i], proj[layer, :, 4 * CHANNELS :], preferred_element_type=jnp.float32
                )
            )
        if layer == 0:
            pl.semaphore_wait(barrier, n - 1)
            for part in range(len(parts)):
                start_edges(layer, part)
        for part, (kind, count) in enumerate(parts):
            send, recv, ret, got = buffers[layer][part]
            wait_all(recv_sem.at[layer, 0, part], recv, arriving(layer, kind)[0])
            own = pl.ds(side * half, half) if (layer, kind) == (0, "half") else slice(None)
            for pair_at in range(send.shape[2]):
                left = recv[own, 0, pair_at].astype(jnp.float32)
                right = recv[:, 1, pair_at].astype(jnp.float32)
                products = []
                for rows in (slice(0, ROWS), slice(ROWS, 2 * ROWS)):
                    product = lax.dot_general(
                        left[:, rows].reshape(-1, TOKENS).astype(jnp.bfloat16),
                        right[:, rows].reshape(-1, TOKENS).astype(jnp.bfloat16),
                        (((1,), (1,)) if layer == 0 else ((0,), (0,)), ((), ())),
                        preferred_element_type=jnp.float32,
                    )
                    products.append(product.reshape(-1, ROWS, TOKENS))
                ret[:, pair_at] = jnp.concatenate(products, axis=1).astype(jnp.bfloat16)
            if (layer, kind) == (0, "half"):
                start_half(ret, got, (layer, 1, part), place)
            else:
                start_group(ret, got, (layer, 1, part))
        if layer == 0:
            for load in loads[4:]:
                load.wait()
        total = jnp.zeros((ROWS, TOKENS), jnp.float32)
        first = 0
        for part, (kind, count) in enumerate(parts):
            got = buffers[layer][part][3]
            wait_all(recv_sem.at[layer, 1, part], got, arriving(layer, kind)[1])
            values = got[...].astype(jnp.float32)
            if (layer, kind) == (1, "half"):
                values = values[:half] + values[half:]
            values = values.reshape(count * ROWS, TOKENS)
            centred[first * ROWS : (first + count) * ROWS] = values
            total += jnp.sum(values.reshape(count, ROWS, TOKENS), axis=0)
            first += count
        average = total / CHANNELS
        shifted = centred[...].reshape(CHANNELS, ROWS, TOKENS) - average[None]
        variance = jnp.mean(shifted * shifted, axis=0)
        scaled = shifted * lax.rsqrt(variance + 1e-05)[None]
        centred[...] = scaled.reshape(CHANNELS * ROWS, TOKENS)
        for i in range(ROWS):
            turned = centred[pl.ds(i, CHANNELS, stride=ROWS), :].T
            product_norm = (turned * out_gain[layer][None] + out_shift[layer][None]).astype(
                jnp.bfloat16
            )
            update = (
                jnp.dot(product_norm, out_weight[layer], preferred_element_type=jnp.float32)
                * gate[i]
            )
            target = current if layer == 0 else out_ref
            target[i] = (source[i].astype(jnp.float32) + update).astype(jnp.bfloat16)
    for layer in range(2):
        for part, (kind, _) in enumerate(PARTS[layer]):
            send, recv, ret, got = buffers[layer][part]
            wait_all(send_sem.at[layer, 0, part], recv, arriving(layer, kind)[0])
            wait_all(send_sem.at[layer, 1, part], got, arriving(layer, kind)[1])


def kernel_body(n, *arrays):
    half = n // 2
    blocks = []
    for layer in range(2):
        for kind, count in PARTS[layer]:
            owners = half if kind == "half" else n
            sources = half if (layer, kind) == (1, "half") else n
            rows = half if (layer, kind) == (0, "half") else n
            tiles = (count // owners // 2, 2 * ROWS, TOKENS)
            blocks += [(owners, 2) + tiles, (sources, 2) + tiles, (rows,) + tiles, (rows,) + tiles]
    return pl.pallas_call(
        functools.partial(kernel, n),
        out_shape=jax.ShapeDtypeStruct((ROWS, TOKENS, CHANNELS), jnp.bfloat16),
        in_specs=[pl.BlockSpec(memory_space=pltpu.HBM)] * 7,
        out_specs=pl.BlockSpec(memory_space=pltpu.VMEM),
        scratch_shapes=[pltpu.VMEM(array.shape, array.dtype) for array in arrays]
        + [
            pltpu.SemaphoreType.DMA((7,)),
            pltpu.VMEM((2, 4 * CHANNELS, CHANNELS), jnp.bfloat16),
            pltpu.VMEM((ROWS, TOKENS, CHANNELS), jnp.bfloat16),
            pltpu.VMEM((ROWS, TOKENS, CHANNELS), jnp.float32),
            pltpu.VMEM((ROWS, TOKENS, CHANNELS), jnp.bfloat16),
            pltpu.VMEM((2, CHANNELS * ROWS, TOKENS), jnp.float32),
            pltpu.VMEM((CHANNELS * ROWS, TOKENS), jnp.float32),
            pltpu.SemaphoreType.DMA((2, 2, max(len(parts) for parts in PARTS))),
            pltpu.SemaphoreType.DMA((2, 2, max(len(parts) for parts in PARTS))),
        ]
        + [pltpu.VMEM(block, jnp.bfloat16) for block in blocks],
        compiler_params=pltpu.CompilerParams(collective_id=0, has_side_effects=True),
    )(*arrays)


def body(pair, *params):
    n = lax.axis_size("row")
    fits = (
        lax.axis_size("col") == 1
        and pair.shape == (ROWS, TOKENS, CHANNELS)
        and n * ROWS == TOKENS
        and n % 4 == 0
        and all(
            count % (2 * (n if kind == "all" else n // 2)) == 0
            for parts in PARTS
            for kind, count in parts
        )
    )
    if fits:
        return kernel_body(n, pair, *params)
    return plain_body(pair, *params)


def solution(mesh):
    placed = (P(("grp", "row"), "col", None), P(), P(), P(), P(), P(), P())
    return jax.shard_map(
        body, mesh=mesh, in_specs=placed, out_specs=P(("grp", "row"), "col", None), check_vma=False
    )
```

```python
import functools

import jax
import jax.numpy as jnp
from jax import lax
from jax.experimental import pallas as pl
from jax.experimental.pallas import tpu as pltpu
from jax.sharding import PartitionSpec as P


def layer_norm(values, scale_vec, offset, axis_pos):
    average = jnp.mean(values, axis=axis_pos, keepdims=True)
    centred = values - average
    variance = jnp.mean(centred * centred, axis=axis_pos, keepdims=True)
    return centred * lax.rsqrt(variance + 1e-05) * scale_vec + offset


def arrange_blocks(arrived, row_count, col_count):
    sources, local_chan, rows_here, cols_here = arrived.shape
    shaped = arrived.reshape(row_count, col_count, local_chan, rows_here, cols_here)
    shaped = shaped.transpose(2, 0, 3, 1, 4)
    return shaped.reshape(local_chan, row_count * rows_here, col_count * cols_here)


def plain_body(pair, in_gain, in_shift, proj, out_gain, out_shift, out_weight):
    rows_here, cols_here, channels = pair.shape
    row_count = lax.axis_size("row")
    col_count = lax.axis_size("col")
    local_chan = channels // (row_count * col_count)
    current = pair
    for layer_index in range(2):
        normed = layer_norm(
            current.astype(jnp.float32), in_gain[layer_index], in_shift[layer_index], 2
        ).astype(jnp.bfloat16)
        weights = proj[layer_index]
        projected = jnp.einsum(
            "ijc,cd->dij", normed, weights[:, : 4 * channels], preferred_element_type=jnp.float32
        )
        left_edge = (
            jax.nn.sigmoid(projected[channels : 2 * channels]) * projected[:channels]
        ).astype(jnp.bfloat16)
        right_edge = (
            jax.nn.sigmoid(projected[3 * channels :]) * projected[2 * channels : 3 * channels]
        ).astype(jnp.bfloat16)
        out_gate = jax.nn.sigmoid(
            jnp.einsum(
                "ijc,cd->ijd",
                normed,
                weights[:, 4 * channels :],
                preferred_element_type=jnp.float32,
            )
        )
        left_arrived, right_arrived = (
            lax.all_to_all(
                left_edge[None], ("row", "col"), split_axis=1, concat_axis=0, tiled=True
            ),
            lax.all_to_all(
                right_edge[None], ("row", "col"), split_axis=1, concat_axis=0, tiled=True
            ),
        )
        left_full = arrange_blocks(left_arrived, row_count, col_count)
        right_full = arrange_blocks(right_arrived, row_count, col_count)
        if layer_index == 0:
            product = jnp.einsum(
                "cik,cjk->cij", left_full, right_full, preferred_element_type=jnp.float32
            )
        else:
            product = jnp.einsum(
                "cki,ckj->cij", left_full, right_full, preferred_element_type=jnp.float32
            )
        product = product.astype(jnp.bfloat16)
        outgoing = product.reshape(local_chan, row_count, rows_here, col_count, cols_here)
        outgoing = outgoing.transpose(1, 3, 0, 2, 4).reshape(
            row_count * col_count, local_chan, rows_here, cols_here
        )
        returned = lax.all_to_all(outgoing, ("row", "col"), split_axis=0, concat_axis=1, tiled=True)
        returned = returned.reshape(channels, rows_here, cols_here)
        product_norm = layer_norm(
            returned.astype(jnp.float32),
            out_gain[layer_index][:, None, None],
            out_shift[layer_index][:, None, None],
            0,
        ).astype(jnp.bfloat16)
        update = (
            jnp.einsum(
                "cij,cd->ijd",
                product_norm,
                out_weight[layer_index],
                preferred_element_type=jnp.float32,
            )
            * out_gate
        )
        current = (current.astype(jnp.float32) + update).astype(jnp.bfloat16)
    return current


PARTS = ((("half", 96), ("half", 32)), (("half", 64), ("all", 64)))
TOKENS = 128
CHANNELS = 128
ROWS = 8


def sigmoid(values):
    return 0.5 * jnp.tanh(0.5 * values) + 0.5


def kernel(n, *refs):
    hbm, out_ref, vmem, rest = refs[:7], refs[7], refs[8:15], refs[15:]
    pair_ref, in_gain, in_shift, proj, out_gain, out_shift, out_weight = vmem
    load_sem, weights_t, normed, gate, current, edges, centred, send_sem, recv_sem = rest[:9]
    buffers, at = [], 9
    for layer in range(2):
        buffers.append([rest[at + 4 * part : at + 4 * part + 4] for part in range(len(PARTS[layer]))])
        at += 4 * len(PARTS[layer])
    me = lax.axis_index("row")
    half = n // 2
    side, place = me // half, lax.rem(me, half)

    def start(source, target, sems, device):
        pltpu.make_async_remote_copy(
            src_ref=source,
            dst_ref=target,
            send_sem=send_sem.at[sems],
            recv_sem=recv_sem.at[sems],
            device_id={"row": device},
            device_id_type=pl.DeviceIdType.MESH,
        ).start()

    def start_group(source, target, sems):
        for offset in range(1, n):
            other = lax.rem(me + offset, n)
            start(source.at[other], target.at[me], sems, other)
        target[me] = source[me]

    def start_half(source, target, sems, slot):
        for offset in range(1, half):
            other = lax.rem(place + offset, half)
            start(source.at[other], target.at[slot], sems, side * half + other)
        target[slot] = source[place]

    def wait_all(sem, buffer, count):
        blocks = buffer.at[pl.ds(0, count)]
        pltpu.make_async_copy(blocks, blocks, sem).wait()

    def arriving(layer, kind):
        if kind == "all":
            return n - 1, n - 1
        return (half // 2 + half - 1, half - 1) if layer == 0 else (half - 1, n - 1)

    def start_edges(layer, part):
        send, recv, _, _ = buffers[layer][part]
        sems = (layer, 0, part)
        if PARTS[layer][part][0] == "all":
            start_group(send, recv, sems)
        elif layer == 0:
            for offset in range(half):
                other = lax.rem(place + offset + 2, half)
                start(send.at[other, 1], recv.at[me, 1], sems, (1 - side) * half + other)
            start_half(send, recv, sems, me)
        else:
            start_half(send, recv, sems, place)

    barrier = pltpu.get_barrier_semaphore()

    def greet(offset, carry):
        pl.semaphore_signal(
            barrier, inc=1, device_id={"row": lax.rem(me + offset, n)},
            device_id_type=pl.DeviceIdType.MESH,
        )
        return carry

    lax.fori_loop(1, n, greet, 0, unroll=True)
    loads = [
        pltpu.make_async_copy(hbm[at], vmem[at], load_sem.at[at]) for at in (0, 3, 1, 2, 4, 5, 6)
    ]
    for load in loads:
        load.start()

    loads[1].wait()
    for layer in range(2):
        for block in range(4):
            columns = proj[layer, :, block * CHANNELS : (block + 1) * CHANNELS]
            turned = columns.astype(jnp.float32).T.astype(jnp.bfloat16)
            first = 0
            for _, count in PARTS[layer]:
                weights_t[layer, pl.ds(4 * first + block * count, count), :] = turned[
                    first : first + count
                ]
                first += count
    for load in (loads[0], loads[2], loads[3]):
        load.wait()
    for layer in range(2):
        parts = PARTS[layer]
        source = pair_ref if layer == 0 else current
        for i in range(ROWS):
            rows = source[i].astype(jnp.float32)
            average = jnp.mean(rows, axis=-1, keepdims=True)
            shifted = rows - average
            variance = jnp.mean(shifted * shifted, axis=-1, keepdims=True)
            normed[i] = (
                shifted * lax.rsqrt(variance + 1e-05) * in_gain[layer][None] + in_shift[layer][None]
            ).astype(jnp.bfloat16)
        first = 0
        for part, (kind, count) in enumerate(parts):
            send, recv, ret, got = buffers[layer][part]
            for i in range(ROWS):
                projected = lax.dot_general(
                    weights_t[layer, pl.ds(4 * first, 4 * count), :],
                    normed[i], (((1,), (1,)), ((), ())),
                    preferred_element_type=jnp.float32,
                )
                p1, p2, p3, p4 = (projected[b * count : (b + 1) * count] for b in range(4))
                edges[0, pl.ds(i, count, stride=ROWS), :] = sigmoid(p2) * p1
                edges[1, pl.ds(i, count, stride=ROWS), :] = sigmoid(p4) * p3
            for edge in range(2):
                send[:, edge] = (
                    edges[edge, : count * ROWS]
                    .astype(jnp.bfloat16)
                    .reshape(send.shape[0], send.shape[2], 2 * ROWS, TOKENS)
                )
            if layer == 1:
                start_edges(layer, part)
            first += count
        for i in range(ROWS):
            gate[i] = sigmoid(
                jnp.dot(
                    normed[i], proj[layer, :, 4 * CHANNELS :], preferred_element_type=jnp.float32
                )
            )
        if layer == 0:
            pl.semaphore_wait(barrier, n - 1)
            for part in range(len(parts)):
                start_edges(layer, part)
        for part, (kind, count) in enumerate(parts):
            send, recv, ret, got = buffers[layer][part]
            wait_all(recv_sem.at[layer, 0, part], recv, arriving(layer, kind)[0])
            own = pl.ds(side * half, half) if (layer, kind) == (0, "half") else slice(None)
            for pair_at in range(send.shape[2]):
                left = recv[own, 0, pair_at].astype(jnp.float32)
                right = recv[:, 1, pair_at].astype(jnp.float32)
                products = []
                for rows in (slice(0, ROWS), slice(ROWS, 2 * ROWS)):
                    product = lax.dot_general(
                        left[:, rows].reshape(-1, TOKENS).astype(jnp.bfloat16),
                        right[:, rows].reshape(-1, TOKENS).astype(jnp.bfloat16),
                        (((1,), (1,)) if layer == 0 else ((0,), (0,)), ((), ())),
                        preferred_element_type=jnp.float32,
                    )
                    products.append(product.reshape(-1, ROWS, TOKENS))
                ret[:, pair_at] = jnp.concatenate(products, axis=1).astype(jnp.bfloat16)
            if (layer, kind) == (0, "half"):
                start_half(ret, got, (layer, 1, part), place)
            else:
                start_group(ret, got, (layer, 1, part))
        if layer == 0:
            for load in loads[4:]:
                load.wait()
        total = jnp.zeros((ROWS, TOKENS), jnp.float32)
        first = 0
        for part, (kind, count) in enumerate(parts):
            got = buffers[layer][part][3]
            wait_all(recv_sem.at[layer, 1, part], got, arriving(layer, kind)[1])
            values = got[...].astype(jnp.float32)
            if (layer, kind) == (1, "half"):
                values = values[:half] + values[half:]
            values = values.reshape(count * ROWS, TOKENS)
            centred[first * ROWS : (first + count) * ROWS] = values
            total += jnp.sum(values.reshape(count, ROWS, TOKENS), axis=0)
            first += count
        average = total / CHANNELS
        shifted = centred[...].reshape(CHANNELS, ROWS, TOKENS) - average[None]
        variance = jnp.mean(shifted * shifted, axis=0)
        scaled = shifted * lax.rsqrt(variance + 1e-05)[None]
        centred[...] = scaled.reshape(CHANNELS * ROWS, TOKENS)
        for i in range(ROWS):
            turned = centred[pl.ds(i, CHANNELS, stride=ROWS), :].T
            product_norm = (turned * out_gain[layer][None] + out_shift[layer][None]).astype(
                jnp.bfloat16
            )
            update = (
                jnp.dot(product_norm, out_weight[layer], preferred_element_type=jnp.float32)
                * gate[i]
            )
            target = current if layer == 0 else out_ref
            target[i] = (source[i].astype(jnp.float32) + update).astype(jnp.bfloat16)
    for layer in range(2):
        for part, (kind, _) in enumerate(PARTS[layer]):
            send, recv, ret, got = buffers[layer][part]
            wait_all(send_sem.at[layer, 0, part], recv, arriving(layer, kind)[0])
            wait_all(send_sem.at[layer, 1, part], got, arriving(layer, kind)[1])


def kernel_body(n, *arrays):
    half = n // 2
    blocks = []
    for layer in range(2):
        for kind, count in PARTS[layer]:
            owners = half if kind == "half" else n
            sources = half if (layer, kind) == (1, "half") else n
            rows = half if (layer, kind) == (0, "half") else n
            tiles = (count // owners // 2, 2 * ROWS, TOKENS)
            blocks += [(owners, 2) + tiles, (sources, 2) + tiles, (rows,) + tiles, (rows,) + tiles]
    return pl.pallas_call(
        functools.partial(kernel, n),
        out_shape=jax.ShapeDtypeStruct((ROWS, TOKENS, CHANNELS), jnp.bfloat16),
        in_specs=[pl.BlockSpec(memory_space=pltpu.HBM)] * 7,
        out_specs=pl.BlockSpec(memory_space=pltpu.VMEM),
        scratch_shapes=[pltpu.VMEM(array.shape, array.dtype) for array in arrays]
        + [
            pltpu.SemaphoreType.DMA((7,)),
            pltpu.VMEM((2, 4 * CHANNELS, CHANNELS), jnp.bfloat16),
            pltpu.VMEM((ROWS, TOKENS, CHANNELS), jnp.bfloat16),
            pltpu.VMEM((ROWS, TOKENS, CHANNELS), jnp.float32),
            pltpu.VMEM((ROWS, TOKENS, CHANNELS), jnp.bfloat16),
            pltpu.VMEM((2, CHANNELS * ROWS, TOKENS), jnp.float32),
            pltpu.VMEM((CHANNELS * ROWS, TOKENS), jnp.float32),
            pltpu.SemaphoreType.DMA((2, 2, max(len(parts) for parts in PARTS))),
            pltpu.SemaphoreType.DMA((2, 2, max(len(parts) for parts in PARTS))),
        ]
        + [pltpu.VMEM(block, jnp.bfloat16) for block in blocks],
        compiler_params=pltpu.CompilerParams(collective_id=0, has_side_effects=True),
    )(*arrays)


def body(pair, *params):
    n = lax.axis_size("row")
    fits = (
        lax.axis_size("col") == 1
        and pair.shape == (ROWS, TOKENS, CHANNELS)
        and n * ROWS == TOKENS
        and n % 4 == 0
        and all(
            count % (2 * (n if kind == "all" else n // 2)) == 0
            for parts in PARTS
            for kind, count in parts
        )
    )
    if fits:
        return kernel_body(n, pair, *params)
    return plain_body(pair, *params)


def solution(mesh):
    placed = (P(("grp", "row"), "col", None), P(), P(), P(), P(), P(), P())
    return jax.shard_map(
        body, mesh=mesh, in_specs=placed, out_specs=P(("grp", "row"), "col", None), check_vma=False
    )
```

```python
import functools

import jax
import jax.numpy as jnp
from jax import lax
from jax.experimental import pallas as pl
from jax.experimental.pallas import tpu as pltpu
from jax.sharding import PartitionSpec as P


def layer_norm(values, scale_vec, offset, axis_pos):
    average = jnp.mean(values, axis=axis_pos, keepdims=True)
    centred = values - average
    variance = jnp.mean(centred * centred, axis=axis_pos, keepdims=True)
    return centred * lax.rsqrt(variance + 1e-05) * scale_vec + offset


def arrange_blocks(arrived, row_count, col_count):
    sources, local_chan, rows_here, cols_here = arrived.shape
    shaped = arrived.reshape(row_count, col_count, local_chan, rows_here, cols_here)
    shaped = shaped.transpose(2, 0, 3, 1, 4)
    return shaped.reshape(local_chan, row_count * rows_here, col_count * cols_here)


def plain_body(pair, in_gain, in_shift, proj, out_gain, out_shift, out_weight):
    rows_here, cols_here, channels = pair.shape
    row_count = lax.axis_size("row")
    col_count = lax.axis_size("col")
    local_chan = channels // (row_count * col_count)
    current = pair
    for layer_index in range(2):
        normed = layer_norm(
            current.astype(jnp.float32), in_gain[layer_index], in_shift[layer_index], 2
        ).astype(jnp.bfloat16)
        weights = proj[layer_index]
        projected = jnp.einsum(
            "ijc,cd->dij", normed, weights[:, : 4 * channels], preferred_element_type=jnp.float32
        )
        left_edge = (
            jax.nn.sigmoid(projected[channels : 2 * channels]) * projected[:channels]
        ).astype(jnp.bfloat16)
        right_edge = (
            jax.nn.sigmoid(projected[3 * channels :]) * projected[2 * channels : 3 * channels]
        ).astype(jnp.bfloat16)
        out_gate = jax.nn.sigmoid(
            jnp.einsum(
                "ijc,cd->ijd",
                normed,
                weights[:, 4 * channels :],
                preferred_element_type=jnp.float32,
            )
        )
        left_arrived, right_arrived = (
            lax.all_to_all(
                left_edge[None], ("row", "col"), split_axis=1, concat_axis=0, tiled=True
            ),
            lax.all_to_all(
                right_edge[None], ("row", "col"), split_axis=1, concat_axis=0, tiled=True
            ),
        )
        left_full = arrange_blocks(left_arrived, row_count, col_count)
        right_full = arrange_blocks(right_arrived, row_count, col_count)
        if layer_index == 0:
            product = jnp.einsum(
                "cik,cjk->cij", left_full, right_full, preferred_element_type=jnp.float32
            )
        else:
            product = jnp.einsum(
                "cki,ckj->cij", left_full, right_full, preferred_element_type=jnp.float32
            )
        product = product.astype(jnp.bfloat16)
        outgoing = product.reshape(local_chan, row_count, rows_here, col_count, cols_here)
        outgoing = outgoing.transpose(1, 3, 0, 2, 4).reshape(
            row_count * col_count, local_chan, rows_here, cols_here
        )
        returned = lax.all_to_all(outgoing, ("row", "col"), split_axis=0, concat_axis=1, tiled=True)
        returned = returned.reshape(channels, rows_here, cols_here)
        product_norm = layer_norm(
            returned.astype(jnp.float32),
            out_gain[layer_index][:, None, None],
            out_shift[layer_index][:, None, None],
            0,
        ).astype(jnp.bfloat16)
        update = (
            jnp.einsum(
                "cij,cd->ijd",
                product_norm,
                out_weight[layer_index],
                preferred_element_type=jnp.float32,
            )
            * out_gate
        )
        current = (current.astype(jnp.float32) + update).astype(jnp.bfloat16)
    return current


PARTS = ((("half", 96), ("half", 32)), (("half", 64), ("all", 64)))
TOKENS = 128
CHANNELS = 128
ROWS = 8


def sigmoid(values):
    return 0.5 * jnp.tanh(0.5 * values) + 0.5


def kernel(n, *refs):
    hbm, out_ref, vmem, rest = refs[:7], refs[7], refs[8:15], refs[15:]
    pair_ref, in_gain, in_shift, proj, out_gain, out_shift, out_weight = vmem
    load_sem, weights_t, normed, gate, current, edges, centred, send_sem, recv_sem = rest[:9]
    buffers, at = [], 9
    for layer in range(2):
        buffers.append([rest[at + 4 * part : at + 4 * part + 4] for part in range(len(PARTS[layer]))])
        at += 4 * len(PARTS[layer])
    me = lax.axis_index("row")
    half = n // 2
    side, place = me // half, lax.rem(me, half)

    def start(source, target, sems, device):
        pltpu.make_async_remote_copy(
            src_ref=source,
            dst_ref=target,
            send_sem=send_sem.at[sems],
            recv_sem=recv_sem.at[sems],
            device_id={"row": device},
            device_id_type=pl.DeviceIdType.MESH,
        ).start()

    def start_group(source, target, sems):
        for offset in range(1, n):
            other = lax.rem(me + offset, n)
            start(source.at[other], target.at[me], sems, other)
        target[me] = source[me]

    def start_half(source, target, sems, slot):
        for offset in (2, 3, 4, 5, 6, 7, 1):
            other = lax.rem(place + offset, half)
            start(source.at[other], target.at[slot], sems, side * half + other)
        target[slot] = source[place]

    def wait_all(sem, buffer, count):
        blocks = buffer.at[pl.ds(0, count)]
        pltpu.make_async_copy(blocks, blocks, sem).wait()

    def arriving(layer, kind):
        if kind == "all":
            return n - 1, n - 1
        return (half // 2 + half - 1, half - 1) if layer == 0 else (half - 1, n - 1)

    def start_edges(layer, part):
        send, recv, _, _ = buffers[layer][part]
        sems = (layer, 0, part)
        if PARTS[layer][part][0] == "all":
            start_group(send, recv, sems)
        elif layer == 0:
            for offset in range(half):
                other = lax.rem(place + offset + 2, half)
                start(send.at[other, 1], recv.at[me, 1], sems, (1 - side) * half + other)
            start_half(send, recv, sems, me)
        else:
            start_half(send, recv, sems, place)

    barrier = pltpu.get_barrier_semaphore()

    def greet(offset, carry):
        pl.semaphore_signal(
            barrier, inc=1, device_id={"row": lax.rem(me + offset, n)},
            device_id_type=pl.DeviceIdType.MESH,
        )
        return carry

    lax.fori_loop(1, n, greet, 0, unroll=True)
    loads = [
        pltpu.make_async_copy(hbm[at], vmem[at], load_sem.at[at]) for at in (0, 3, 1, 2, 4, 5, 6)
    ]
    for load in loads:
        load.start()

    loads[1].wait()
    for layer in range(2):
        for block in range(4):
            columns = proj[layer, :, block * CHANNELS : (block + 1) * CHANNELS]
            turned = columns.astype(jnp.float32).T.astype(jnp.bfloat16)
            first = 0
            for _, count in PARTS[layer]:
                weights_t[layer, pl.ds(4 * first + block * count, count), :] = turned[
                    first : first + count
                ]
                first += count
    for load in (loads[0], loads[2], loads[3]):
        load.wait()
    for layer in range(2):
        parts = PARTS[layer]
        source = pair_ref if layer == 0 else current
        for i in range(ROWS):
            rows = source[i].astype(jnp.float32)
            average = jnp.mean(rows, axis=-1, keepdims=True)
            shifted = rows - average
            variance = jnp.mean(shifted * shifted, axis=-1, keepdims=True)
            normed[i] = (
                shifted * lax.rsqrt(variance + 1e-05) * in_gain[layer][None] + in_shift[layer][None]
            ).astype(jnp.bfloat16)
        first = 0
        for part, (kind, count) in enumerate(parts):
            send, recv, ret, got = buffers[layer][part]
            for i in range(ROWS):
                projected = lax.dot_general(
                    weights_t[layer, pl.ds(4 * first, 4 * count), :],
                    normed[i], (((1,), (1,)), ((), ())),
                    preferred_element_type=jnp.float32,
                )
                p1, p2, p3, p4 = (projected[b * count : (b + 1) * count] for b in range(4))
                edges[0, pl.ds(i, count, stride=ROWS), :] = sigmoid(p2) * p1
                edges[1, pl.ds(i, count, stride=ROWS), :] = sigmoid(p4) * p3
            for edge in range(2):
                send[:, edge] = (
                    edges[edge, : count * ROWS]
                    .astype(jnp.bfloat16)
                    .reshape(send.shape[0], send.shape[2], 2 * ROWS, TOKENS)
                )
            if layer == 1:
                start_edges(layer, part)
            first += count
        for i in range(ROWS):
            gate[i] = sigmoid(
                jnp.dot(
                    normed[i], proj[layer, :, 4 * CHANNELS :], preferred_element_type=jnp.float32
                )
            )
        if layer == 0:
            pl.semaphore_wait(barrier, n - 1)
            for part in range(len(parts)):
                start_edges(layer, part)
        for part, (kind, count) in enumerate(parts):
            send, recv, ret, got = buffers[layer][part]
            wait_all(recv_sem.at[layer, 0, part], recv, arriving(layer, kind)[0])
            own = pl.ds(side * half, half) if (layer, kind) == (0, "half") else slice(None)
            for pair_at in range(send.shape[2]):
                left = recv[own, 0, pair_at].astype(jnp.float32)
                right = recv[:, 1, pair_at].astype(jnp.float32)
                products = []
                for rows in (slice(0, ROWS), slice(ROWS, 2 * ROWS)):
                    product = lax.dot_general(
                        left[:, rows].reshape(-1, TOKENS).astype(jnp.bfloat16),
                        right[:, rows].reshape(-1, TOKENS).astype(jnp.bfloat16),
                        (((1,), (1,)) if layer == 0 else ((0,), (0,)), ((), ())),
                        preferred_element_type=jnp.float32,
                    )
                    products.append(product.reshape(-1, ROWS, TOKENS))
                ret[:, pair_at] = jnp.concatenate(products, axis=1).astype(jnp.bfloat16)
            if (layer, kind) == (0, "half"):
                start_half(ret, got, (layer, 1, part), place)
            else:
                start_group(ret, got, (layer, 1, part))
        if layer == 0:
            for load in loads[4:]:
                load.wait()
        total = jnp.zeros((ROWS, TOKENS), jnp.float32)
        first = 0
        for part, (kind, count) in enumerate(parts):
            got = buffers[layer][part][3]
            wait_all(recv_sem.at[layer, 1, part], got, arriving(layer, kind)[1])
            values = got[...].astype(jnp.float32)
            if (layer, kind) == (1, "half"):
                values = values[:half] + values[half:]
            values = values.reshape(count * ROWS, TOKENS)
            centred[first * ROWS : (first + count) * ROWS] = values
            total += jnp.sum(values.reshape(count, ROWS, TOKENS), axis=0)
            first += count
        average = total / CHANNELS
        shifted = centred[...].reshape(CHANNELS, ROWS, TOKENS) - average[None]
        variance = jnp.mean(shifted * shifted, axis=0)
        scaled = shifted * lax.rsqrt(variance + 1e-05)[None]
        centred[...] = scaled.reshape(CHANNELS * ROWS, TOKENS)
        for i in range(ROWS):
            turned = centred[pl.ds(i, CHANNELS, stride=ROWS), :].T
            product_norm = (turned * out_gain[layer][None] + out_shift[layer][None]).astype(
                jnp.bfloat16
            )
            update = (
                jnp.dot(product_norm, out_weight[layer], preferred_element_type=jnp.float32)
                * gate[i]
            )
            target = current if layer == 0 else out_ref
            target[i] = (source[i].astype(jnp.float32) + update).astype(jnp.bfloat16)
    for layer in range(2):
        for part, (kind, _) in enumerate(PARTS[layer]):
            send, recv, ret, got = buffers[layer][part]
            wait_all(send_sem.at[layer, 0, part], recv, arriving(layer, kind)[0])
            wait_all(send_sem.at[layer, 1, part], got, arriving(layer, kind)[1])


def kernel_body(n, *arrays):
    half = n // 2
    blocks = []
    for layer in range(2):
        for kind, count in PARTS[layer]:
            owners = half if kind == "half" else n
            sources = half if (layer, kind) == (1, "half") else n
            rows = half if (layer, kind) == (0, "half") else n
            tiles = (count // owners // 2, 2 * ROWS, TOKENS)
            blocks += [(owners, 2) + tiles, (sources, 2) + tiles, (rows,) + tiles, (rows,) + tiles]
    return pl.pallas_call(
        functools.partial(kernel, n),
        out_shape=jax.ShapeDtypeStruct((ROWS, TOKENS, CHANNELS), jnp.bfloat16),
        in_specs=[pl.BlockSpec(memory_space=pltpu.HBM)] * 7,
        out_specs=pl.BlockSpec(memory_space=pltpu.VMEM),
        scratch_shapes=[pltpu.VMEM(array.shape, array.dtype) for array in arrays]
        + [
            pltpu.SemaphoreType.DMA((7,)),
            pltpu.VMEM((2, 4 * CHANNELS, CHANNELS), jnp.bfloat16),
            pltpu.VMEM((ROWS, TOKENS, CHANNELS), jnp.bfloat16),
            pltpu.VMEM((ROWS, TOKENS, CHANNELS), jnp.float32),
            pltpu.VMEM((ROWS, TOKENS, CHANNELS), jnp.bfloat16),
            pltpu.VMEM((2, CHANNELS * ROWS, TOKENS), jnp.float32),
            pltpu.VMEM((CHANNELS * ROWS, TOKENS), jnp.float32),
            pltpu.SemaphoreType.DMA((2, 2, max(len(parts) for parts in PARTS))),
            pltpu.SemaphoreType.DMA((2, 2, max(len(parts) for parts in PARTS))),
        ]
        + [pltpu.VMEM(block, jnp.bfloat16) for block in blocks],
        compiler_params=pltpu.CompilerParams(collective_id=0, has_side_effects=True),
    )(*arrays)


def body(pair, *params):
    n = lax.axis_size("row")
    fits = (
        lax.axis_size("col") == 1
        and pair.shape == (ROWS, TOKENS, CHANNELS)
        and n * ROWS == TOKENS
        and n % 4 == 0
        and all(
            count % (2 * (n if kind == "all" else n // 2)) == 0
            for parts in PARTS
            for kind, count in parts
        )
    )
    if fits:
        return kernel_body(n, pair, *params)
    return plain_body(pair, *params)


def solution(mesh):
    placed = (P(("grp", "row"), "col", None), P(), P(), P(), P(), P(), P())
    return jax.shard_map(
        body, mesh=mesh, in_specs=placed, out_specs=P(("grp", "row"), "col", None), check_vma=False
    )
```
